512 devices in a mesh: tm: 16 (over z, core), space: 32 (over x, y).
Axes of the slice: x: 4, y: 8, z: 8, core: 2. Of those that a mesh axis runs over, the one named last changes fastest.
Arguments:
- iterate: float32 [16, 32, 16, 16, 512], P('tm', 'space'), may hold values from -3 to 3
- source_term: float32 [16, 32, 16, 16, 512], P('tm', 'space'), may hold values from -6 to 6
- conductivity: float32 [32, 16, 16, 512], P('space'), may hold values from 0.5 to 4
Outputs:
- new_iterate: float32 [16, 32, 16, 16, 512], P('tm', 'space')
- residual: float32 [16, 32, 16, 16, 512], P('tm', 'space')
The draws below stay inside these ranges and needn't reach their ends.
All inputs are finite; a program needn't handle non-finite values.
Results may differ from the reference program's by a relative error of at most 0.00002.
Values sent between devices are 32-bit elements; how exact they have to be, the bound alone decides.
No kernel may reach another device: no remote copies, remote signals or barrier semaphores. Data moves between devices by JAX's collectives and lax.ppermute only.
A program may use at most 64 MiB of HBM per device.

```python
import math
import jax
import jax.numpy as jnp

NZ = 16
TX = 16
TY = 512
TILES = 32
NT = 16
N_SPACE = 32


def level_of(own_key, dims, split, smallest, top_value):
    def one(dim, parts):
        draws = jax.random.uniform(jax.random.fold_in(jax.random.fold_in(own_key, 6), dim), (parts,), jnp.float32, smallest / len(split), top_value / len(split))
        return jnp.repeat(jnp.exp(draws), dims[dim] // parts).reshape((-1,) + (1,) * (len(dims) - dim - 1))

    factor_of = one(*split[0])
    for cut in split[1:]:
        factor_of = factor_of * one(*cut)
    return factor_of


def bell_draw(own_key, extent, scale, most, split=(), dtype=jnp.bfloat16):
    loudness = level_of(own_key, extent, split, -0.22, 0.18) if split else 1.0
    array = jax.random.normal(own_key, extent, jnp.float32) * scale * loudness
    return jnp.minimum(jnp.maximum(array, -most), most).astype(dtype)


def setup_inputs(seed: int = 0) -> dict:
    key_of = jax.random.split(jax.random.key(seed), 4)
    return {
        "iterate": bell_draw(key_of[0], (NT, TILES, NZ, TX, TY), 0.6, 3.0, ((0, 16), (1, 32)), jnp.float32),
        "source_term": bell_draw(key_of[1], (NT, TILES, NZ, TX, TY), 1.0, 6.0, ((0, 16), (1, 32)), jnp.float32),
        "conductivity": jnp.clip(jnp.exp(math.log(4.0) - 2.0794415 * jax.random.uniform(key_of[2], (TILES, NZ, TX, TY), jnp.float32) ** level_of(key_of[2], (TILES, NZ, TX, TY), ((0, 32),), -0.2, 0.2)), 0.5, 4.0),
    }


tau_step = 0.08
damping = 0.7


def to_grid(tiled):
    frames = tiled.shape[0]
    return tiled.transpose(0, 2, 1, 3, 4).reshape(frames, NZ, N_SPACE * TX, TY)


def from_grid(grid_field):
    frames = grid_field.shape[0]
    shaped = grid_field.reshape(frames, NZ, N_SPACE, TX, TY)
    return shaped.transpose(0, 2, 1, 3, 4)


def neighbours(grid_field):
    padded = jnp.pad(grid_field, ((0, 0), (1, 1), (1, 1), (1, 1)))
    return [padded[:, 1:-1, :-2, 1:-1], padded[:, 1:-1, 2:, 1:-1],
            padded[:, 1:-1, 1:-1, :-2], padded[:, 1:-1, 1:-1, 2:],
            padded[:, :-2, 1:-1, 1:-1], padded[:, 2:, 1:-1, 1:-1]]


def face_weights(conduct):
    weights = [0.5 * (conduct + other) for other in neighbours(conduct)]
    weight_sum = weights[0]
    for near_item in weights[1:]:
        weight_sum = weight_sum + near_item
    return weights, weight_sum


def earlier(grid_field):
    return jnp.concatenate([jnp.zeros_like(grid_field[:1]), grid_field[:-1]], axis=0)


def apply_operator(update, weights, weight_sum, step_size):
    near_list = neighbours(update)
    flux_sum = weights[0] * near_list[0]
    for position in range(1, 6):
        flux_sum = flux_sum + weights[position] * near_list[position]
    return update - earlier(update) + step_size * (weight_sum * update - flux_sum)


def smooth(rhs_field, weights, weight_sum, step_size, want_left):
    diag_term = 1.0 + step_size * weight_sum
    update = damping * rhs_field / diag_term
    update = update + damping * (rhs_field - apply_operator(update, weights, weight_sum, step_size)) / diag_term
    if want_left:
        return update, rhs_field - apply_operator(update, weights, weight_sum, step_size)
    return update, update


def reference(iterate, source_term, conductivity):
    state_grid = to_grid(iterate)
    source_grid = to_grid(source_term)
    kappa_grid = to_grid(conductivity[None])
    conduct = kappa_grid * (1.0 + state_grid * state_grid)
    weights, weight_sum = face_weights(conduct)
    residual = source_grid - apply_operator(state_grid, weights, weight_sum, tau_step)
    fine_update, fine_left = smooth(residual, weights, weight_sum, tau_step, True)
    mid_rhs = fine_left[0::2] + fine_left[1::2]
    mid_conduct = 0.5 * (conduct[0::2] + conduct[1::2])
    weights, weight_sum = face_weights(mid_conduct)
    mid_update, mid_left = smooth(mid_rhs, weights, weight_sum, 2.0 * tau_step, True)
    top_rhs = mid_left[0::2] + mid_left[1::2]
    top_conduct = 0.5 * (mid_conduct[0::2] + mid_conduct[1::2])
    weights, weight_sum = face_weights(top_conduct)
    top_update, unused = smooth(top_rhs, weights, weight_sum, 4.0 * tau_step, False)
    mid_update = mid_update + jnp.repeat(top_update, 2, axis=0)
    fine_update = fine_update + jnp.repeat(mid_update, 2, axis=0)
    return from_grid(state_grid + fine_update), from_grid(residual)
```

```python
import jax
import jax.numpy as jnp
from jax import lax
from jax.sharding import PartitionSpec as P

tau = 0.08
omega = 0.7


def routes(chips, slabs):
    def device(z, core, slab):
        return (2 * z + core) * slabs + slab

    every = [(z, c, s) for z in range(chips) for c in range(2) for s in range(slabs)]
    pair = [(device(z, c, s), device(z, 1 - c, s)) for z, c, s in every]
    outer = []
    for z, c, s in every:
        near = s - 1 if c == 0 else s + 1
        if 0 <= near < slabs:
            outer.append((device(z, c, s), device(z, 1 - c, near)))
    later = [(device(z, c, s), device(z + 1, c, s)) for z, c, s in every if z + 1 < chips]
    later2 = [(device(z, c, s), device(z + 2, c, s)) for z, c, s in every if z + 2 < chips]
    twin = [(device(z, c, s), device(z ^ 1, c, s)) for z, c, s in every]
    return pair, outer, later, later2, twin


def weights_of(c):
    mid = c[:, 1:-1]
    near = [c[:, :-2], c[:, 2:]] + flat_near(mid)
    weights = [0.5 * (mid + other) for other in near]
    total = weights[0]
    for w in weights[1:]:
        total = total + w
    return weights, total


def flat_near(v):
    zero_y = jnp.zeros_like(v[..., :1])
    zero_z = jnp.zeros_like(v[..., :1, :])
    return [
        jnp.concatenate([zero_y, v[..., :-1]], -1),
        jnp.concatenate([v[..., 1:], zero_y], -1),
        jnp.concatenate([zero_z, v[..., :-1, :]], -2),
        jnp.concatenate([v[..., 1:, :], zero_z], -2),
    ]


def operator(v, before, after, prev, weights, total, step):
    low = jnp.concatenate([before, v[:, :-1]], 1)
    high = jnp.concatenate([v[:, 1:], after], 1)
    near = [low, high] + flat_near(v)
    flux = weights[0] * near[0]
    for w, n in zip(weights[1:], near[1:]):
        flux = flux + w * n
    return v - prev + step * (total * v - flux)


def solution(mesh):
    slabs = mesh.shape["space"]
    chips = mesh.shape["tm"] // 2
    pair, outer, later, later2, twin = routes(chips, slabs)
    axes = ("tm", "space")

    def send(x, route):
        return lax.ppermute(x, axes, route)

    def shards(iterate, source_term, conductivity):
        core = lax.axis_index("tm") % 2
        first = core == 0

        def rows(a):
            a = jnp.swapaxes(a, 0, 1)
            return jnp.where(first, a, a[::-1])

        u_own = rows(iterate[0, 0])
        f_own = rows(source_term[0, 0])
        kappa = rows(conductivity[0])
        got = send(jnp.concatenate([u_own[7:][::-1], f_own[8:][::-1]], 0), pair)

        def both(own, other):
            return jnp.where(first, jnp.stack([own, other]), jnp.stack([other, own]))

        u = both(u_own[:9], got[:9])
        f = both(f_own[:8], got[9:])
        u_prev = send(u[1, :8], later)
        edge = send(jnp.concatenate([u[:, 0], kappa[:1]], 0), outer)
        u_all = jnp.concatenate([edge[:2, None], u], 1)
        kappa_all = jnp.concatenate([edge[2:], kappa[:9]], 0)
        c = kappa_all[None] * (1.0 + u_all * u_all)
        w, total = weights_of(c)
        u_mid = u_all[:, 1:-1]
        prev = jnp.stack([u_prev, u_mid[0]])
        b = f - operator(u_mid, u_all[:, :1], u_all[:, -1:], prev, w, total, tau)
        diag = 1.0 + tau * total
        e0 = omega * b / diag

        def exchange(v):
            return send(v[:, 0], outer)[:, None], send(v[:, -1], pair)[:, None]

        z0 = send(e0[1], later)
        o0, i0 = exchange(e0)
        e1 = e0 + omega * (b - operator(e0, o0, i0, jnp.stack([z0, e0[0]]), w, total, tau)) / diag
        z1 = send(e1[1], later)
        o1, i1 = exchange(e1)
        r = b - operator(e1, o1, i1, jnp.stack([z1, e1[0]]), w, total, tau)

        bm = (r[0] + r[1])[None]
        cm = (0.5 * (c[0] + c[1]))[None]
        wm, totalm = weights_of(cm)
        cm_twin = send(cm, twin)
        diagm = 1.0 + 2 * tau * totalm
        m0 = omega * bm / diagm
        zm0 = send(m0, later)
        o, i = exchange(m0)
        m1 = m0 + omega * (bm - operator(m0, o, i, zm0, wm, totalm, 2 * tau)) / diagm
        zm1 = send(m1, later)
        o, i = exchange(m1)
        rm = bm - operator(m1, o, i, zm1, wm, totalm, 2 * tau)

        bt = rm + send(rm, twin)
        ct = 0.5 * (cm + cm_twin)
        wt, totalt = weights_of(ct)
        diagt = 1.0 + 4 * tau * totalt
        t0 = omega * bt / diagt
        zt0 = send(t0, later2)
        o, i = exchange(t0)
        t1 = t0 + omega * (bt - operator(t0, o, i, zt0, wt, totalt, 4 * tau)) / diagt
        update = e1 + (m1 + t1)

        def mine(x):
            return jnp.where(first, x[0], x[1]), jnp.where(first, x[1], x[0])

        own_up, other_up = mine(update)
        own_b, other_b = mine(b)
        got_b = send(other_b, pair)
        got_up = send(other_up, pair)

        def natural(own, got):
            a = jnp.concatenate([own, got[::-1]], 0)
            return jnp.swapaxes(jnp.where(first, a, a[::-1]), 0, 1)

        new = iterate[0, 0] + natural(own_up, got_up)
        return new[None, None], natural(own_b, got_b)[None, None]

    spec = P("tm", "space", None, None, None)
    return jax.shard_map(
        shards,
        mesh=mesh,
        in_specs=(spec, spec, P("space", None, None, None)),
        out_specs=(spec, spec),
        check_vma=False,
    )
```

```python
import functools
import jax
import jax.numpy as jnp
from jax import lax
from jax.experimental import pallas as pl
from jax.experimental.pallas import tpu as pltpu
from jax.sharding import PartitionSpec as P

tau = 0.08
omega = 0.7
keep = 1.0 - omega


def routes(chips, slabs):
    def device(z, core, slab):
        return (2 * z + core) * slabs + slab

    every = [(z, c, s) for z in range(chips) for c in range(2) for s in range(slabs)]
    pair = [(device(z, c, s), device(z, 1 - c, s)) for z, c, s in every]
    outer = []
    for z, c, s in every:
        near = s - 1 if c == 0 else s + 1
        if 0 <= near < slabs:
            outer.append((device(z, c, s), device(z, 1 - c, near)))
    later = [(device(z, c, s), device(z + 1, c, s)) for z, c, s in every if z + 1 < chips]
    later2 = [(device(z, c, s), device(z + 2, c, s)) for z, c, s in every if z + 2 < chips]
    twin = [(device(z, c, s), device(z ^ 1, c, s)) for z, c, s in every]
    in_chip = [[device(z, 0, s), device(z, 1, s)] for z in range(chips) for s in range(slabs)]
    twins = [
        [device(2 * k, c, s), device(2 * k + 1, c, s)]
        for k in range(chips // 2)
        for c in range(2)
        for s in range(slabs)
    ]
    return pair, outer, later, later2, twin, in_chip, twins


def iota(v, axis):
    return lax.broadcasted_iota(jnp.int32, v.shape, axis)


def around(v):
    ny = v.shape[1]
    nz = v.shape[0]
    return (
        pltpu.roll(v, 1, 1),
        pltpu.roll(v, ny - 1, 1),
        pltpu.roll(v, 1, 0),
        pltpu.roll(v, nz - 1, 0),
    )


def faces(c, low, high, step):
    ny = c.shape[1]
    nz = c.shape[0]
    y = iota(c, 1)
    z = iota(c, 0)
    inside = (y > 0, y < ny - 1, z > 0, z < nz - 1)
    near = [jnp.where(ok, n, 0.0) for ok, n in zip(inside, around(c))]
    total = low + high
    for n in near:
        total = total + n
    diag = 1.0 + step * (3.0 * c + 0.5 * total)
    weights = [jnp.where(ok, (0.5 * step) * (c + n), 0.0) for ok, n in zip(inside, near)]
    return weights, (0.5 * step) * (c + high), diag


def spread(v, low, high, weights, w_low, w_high):
    flux = w_low * low + w_high * high
    for w, n in zip(weights, around(v)):
        flux = flux + w * n
    return flux


def k_split(info, u, f, kap, uo, fo, ko, send):
    def rows(mirror):
        for x in range(16):
            row = 15 - x if mirror else x
            if row <= 8:
                value = u[:, x, :]
                uo[row] = value
                ko[row] = kap[:, x, :]
                if row <= 7:
                    fo[row] = f[:, x, :]
            back = 15 - row
            if back <= 8:
                send[back] = u[:, x, :]
                if back <= 7:
                    send[9 + back] = f[:, x, :]

    pl.when(info[0] == 0)(lambda: rows(False))
    pl.when(info[0] == 1)(lambda: rows(True))


def k_pack(info, uo, fo, ko, got, u, f, edge, zu, cm):
    h = info[0]
    for x in range(9):
        u[h, x] = uo[x]
        u[1 - h, x] = got[x]
        cm[x] = (0.5 * ko[x]) * (2.0 + uo[x] * uo[x] + got[x] * got[x])
    for x in range(8):
        f[h, x] = fo[x]
        f[1 - h, x] = got[9 + x]
        zu[x] = u[1, x]
    for x in range(3):
        edge[x] = u[0, x]
        edge[3 + x] = u[1, x]
        edge[6 + x] = ko[x]
    for x in range(2):
        edge[9 + x] = f[0, x]
        edge[11 + x] = f[1, x]


def k_residual(info, u, f, ko, edge, zu, w, wx, diag, gain, b, e0, cm, zpay, ipay, c):
    h = info[0]
    real = info[1] == 1

    def uu(t, x):
        return u[t, x] if x >= 0 else edge[3 * t - x - 1]

    for x in range(-3, 9):
        k = ko[x] if x >= 0 else edge[5 - x]
        for t in range(2):
            v = uu(t, x)
            c[t, x + 3] = k * (1.0 + v * v)
        cm[x + 3] = 0.5 * (c[0, x + 3] + c[1, x + 3])
    for t in range(2):
        wx[t, 0] = (0.5 * tau) * (c[t, 0] + c[t, 1])
        for x in range(-2, 8):
            i = x + 2
            weights, w_high, d = faces(c[t, i + 1], c[t, i], c[t, i + 2], tau)
            wx[t, i + 1] = w_high
            for k in range(4):
                w[k, t, i] = weights[k]
            g = omega / d
            diag[t, i] = d
            gain[t, i] = g
            v = uu(t, x)
            f_row = f[t, x] if x >= 0 else edge[8 + 2 * t - x]
            value = f_row - d * v + spread(v, uu(t, x - 1), uu(t, x + 1), weights, wx[t, i], w_high)
            if t == 1:
                value = value + uu(0, x)
            elif x >= 0:
                value = value + zu[x]
            if x < 0:
                value = jnp.where(real, value, 0.0)
            b[t, i] = value
            e0[t, i] = g * value
    for i in range(9):
        zpay[i] = e0[1, i + 1]
    zpay[9] = edge[3]
    zpay[10] = edge[4]
    ipay[0] = e0[0, 9]
    ipay[1] = e0[1, 9]
    for x in range(8):
        ipay[2 + x] = b[1 - h, x + 2]


def k_fine(info, w, wx, gain, b, e0, z, near, e1, zpay, ipay, v):
    h = info[0]
    real = info[1] == 1
    for t in range(2):
        for i in range(10):
            value = e0[t, i]
            if t == 0 and i < 2:
                value = value + jnp.where(real, gain[t, i] * z[10 - i], 0.0)
            v[t, i] = value
        v[t, 10] = near[1 - h, t]
    for t in range(2):
        for i in range(1, 10):
            here = v[t, i]
            weights = [w[k, t, i] for k in range(4)]
            flux = spread(here, v[t, i - 1], v[t, i + 1], weights, wx[t, i], wx[t, i + 1])
            prev = z[i - 1] if t == 0 else v[0, i]
            right = b[t, i] + prev
            if t == 0 and i == 1:
                right = right + z[9]
            value = keep * here + gain[t, i] * (right + flux)
            if i == 1:
                value = jnp.where(real, value, 0.0)
            e1[t, i - 1] = value
    for x in range(8):
        zpay[x] = e1[1, x + 1]
    ipay[0] = e1[0, 8]
    ipay[1] = e1[1, 8]


def k_mid_faces(cm, cm_twin, w, wx, diag, gain, ct):
    wx[0] = tau * (cm[0] + cm[1])
    for i in range(10):
        weights, w_high, d = faces(cm[i + 1], cm[i], cm[i + 2], 2 * tau)
        wx[i + 1] = w_high
        for k in range(4):
            w[k, i] = weights[k]
        diag[i] = d
        gain[i] = omega / d
    for x in range(9):
        ct[x] = 0.5 * (cm[x + 3] + cm_twin[x])


def k_restrict(info, w, wx, diag, b, e1, z, near, gain_mid, ct, bm, m0, edge, ipay):
    h = info[0]
    for x in range(8):
        i = x + 2
        parts = []
        for t in range(2):
            here = e1[t, x + 1]
            high = e1[t, x + 2] if x < 7 else near[1 - h, t]
            weights = [w[k, t, i] for k in range(4)]
            flux = spread(here, e1[t, x], high, weights, wx[t, i], wx[t, i + 1])
            prev = z[x] if t == 0 else e1[0, x + 1]
            parts.append(b[t, i] - diag[t, i] * here + prev + flux)
        value = parts[0] + parts[1]
        bm[x] = value
        m0[x] = gain_mid[i] * value
    edge[0] = bm[0]
    edge[1] = bm[1]
    edge[2] = ct[0]
    ipay[0] = m0[7]


def k_mid(info, w, wx, gain, bm, m0, edge, z, near, m1, zpay, ipay):
    h = info[0]
    real = info[1] == 1

    def v(x):
        if x < 0:
            return gain[x + 2] * edge[-x - 1]
        return m0[x] if x < 8 else near[1 - h, 0]

    for x in range(-1, 8):
        i = x + 2
        here = v(x)
        weights = [w[k, i] for k in range(4)]
        flux = spread(here, v(x - 1), v(x + 1), weights, wx[i], wx[i + 1])
        right = edge[0] if x < 0 else bm[x] + z[x]
        value = keep * here + gain[i] * (right + flux)
        if x < 0:
            value = jnp.where(real, value, 0.0)
        else:
            zpay[x] = value
        m1[x + 1] = value
    zpay[8] = v(-1)
    ipay[0] = m1[8]


def k_mid_left(info, w, wx, diag, gain, bm, m1, z, near, rm):
    h = info[0]
    real = info[1] == 1

    def v(x):
        if x < 0:
            return m1[0] + jnp.where(real, gain[1] * z[8], 0.0)
        return m1[x + 1] if x < 8 else near[1 - h, 0]

    for x in range(8):
        i = x + 2
        here = v(x)
        weights = [w[k, i] for k in range(4)]
        flux = spread(here, v(x - 1), v(x + 1), weights, wx[i], wx[i + 1])
        rm[x] = bm[x] - diag[i] * here + z[x] + flux


def k_top_faces(ct, edge, w, wx, gain):
    wx[0] = (2 * tau) * (edge[2] + ct[0])
    for x in range(8):
        low = ct[x - 1] if x else edge[2]
        weights, w_high, d = faces(ct[x], low, ct[x + 1], 4 * tau)
        wx[x + 1] = w_high
        for k in range(4):
            w[k, x] = weights[k]
        gain[x] = omega / d


def k_top_start(gain, rm, bt, t0, edge, ipay):
    for x in range(8):
        value = rm[0, x] + rm[1, x]
        bt[x] = value
        t0[x] = gain[x] * value
    edge[0] = t0[0]
    ipay[0] = t0[7]


def k_top(info, w, wx, gain, bt, t0, edge, z, near, m1, e1, mine, other):
    h = info[0]
    for x in range(8):
        here = t0[x]
        low = t0[x - 1] if x else edge[0]
        high = t0[x + 1] if x < 7 else near[1 - h, 0]
        weights = [w[k, x] for k in range(4)]
        flux = spread(here, low, high, weights, wx[x], wx[x + 1])
        value = keep * here + gain[x] * (bt[x] + z[x] + flux)
        value = value + m1[x + 1]
        mine[x] = e1[h, x + 1] + value
        other[x] = e1[1 - h, x + 1] + value


def k_residual_out(info, b, near, out):
    h = info[0]

    def rows(mirror):
        for x in range(16):
            row = 15 - x if mirror else x
            out[:, x, :] = b[h, row + 2] if row < 8 else near[1 - h, 2 + 15 - row]

    pl.when(h == 0)(lambda: rows(False))
    pl.when(h == 1)(lambda: rows(True))


def k_state_out(info, u, mine, got, out):
    h = info[0]

    def rows(mirror):
        for x in range(16):
            row = 15 - x if mirror else x
            out[:, x, :] = u[:, x, :] + (mine[row] if row < 8 else got[15 - row])

    pl.when(h == 0)(lambda: rows(False))
    pl.when(h == 1)(lambda: rows(True))


VMEM = pl.BlockSpec(memory_space=pltpu.VMEM)
SMEM = pl.BlockSpec(memory_space=pltpu.SMEM)


def solution(mesh):
    slabs = mesh.shape["space"]
    chips = mesh.shape["tm"] // 2
    pair, outer, later, later2, twin, in_chip, twins = routes(chips, slabs)
    axes = ("tm", "space")

    def send(x, route):
        return lax.ppermute(x, axes, route)

    def gather(x, groups):
        return lax.all_gather(x, axes, axis_index_groups=groups)

    def call(kernel, shapes, *args, info=None, scratch=(), work=20):
        lead = () if info is None else (info,)
        size = sum(a.size for a in args) * 4
        return pl.pallas_call(
            kernel,
            out_shape=[jax.ShapeDtypeStruct(s + (16, 512), jnp.float32) for s in shapes],
            in_specs=[SMEM] * len(lead) + [VMEM] * len(args),
            out_specs=[VMEM] * len(shapes),
            scratch_shapes=[pltpu.VMEM(s + (16, 512), jnp.float32) for s in scratch],
            cost_estimate=pl.CostEstimate(flops=work * 131072, bytes_accessed=size, transcendentals=0),
            compiler_params=pltpu.CompilerParams(vmem_limit_bytes=24 * 2**20),
            name=kernel.__name__,
        )(*lead, *args)

    def shards(iterate, source_term, conductivity):
        core = lax.axis_index("tm") % 2
        slab = lax.axis_index("space")
        edge_slab = jnp.where(core == 0, 0, slabs - 1)
        info = jnp.stack([core, (slab != edge_slab).astype(jnp.int32)]).astype(jnp.int32)
        u_in = iterate[0, 0]

        uo, fo, ko, pay = call(
            k_split, [(9,), (8,), (9,), (17,)], u_in, source_term[0, 0], conductivity[0], info=info
        )
        got = send(pay, pair)
        u, f, edge, zu, cm_part = call(
            k_pack, [(2, 9), (2, 8), (13,), (8,), (9,)], uo, fo, ko, got, info=info
        )
        edge = send(edge, outer)
        zu = send(zu, later)
        cm_twin = send(cm_part, twin)
        w, wx, diag, gain, b, e0, cm, zpay, ipay = call(
            k_residual,
            [(4, 2, 10), (2, 11), (2, 10), (2, 10), (2, 10), (2, 10), (12,), (11,), (10,)],
            u, f, ko, edge, zu,
            info=info,
            scratch=[(2, 12)],
        )
        z = send(zpay, later)
        near_b = gather(ipay, in_chip)
        e1, zpay, ipay = call(
            k_fine, [(2, 9), (8,), (2,)], w, wx, gain, b, e0, z, near_b, info=info, scratch=[(2, 11)]
        )
        z = send(zpay, later)
        near = gather(ipay, in_chip)
        (residual,) = call(k_residual_out, [(16,)], b, near_b, info=info)
        wm, wxm, diagm, gainm, ct = call(
            k_mid_faces, [(4, 10), (11,), (10,), (10,), (9,)], cm, cm_twin
        )
        bm, m0, pay, ipay = call(
            k_restrict, [(8,), (8,), (3,), (1,)], w, wx, diag, b, e1, z, near, gainm, ct, info=info
        )
        z = send(m0, later)
        edge = send(pay, outer)
        near = gather(ipay, in_chip)
        m1, zpay, ipay = call(
            k_mid, [(9,), (9,), (1,)], wm, wxm, gainm, bm, m0, edge, z, near, info=info
        )
        z = send(zpay, later)
        near = gather(ipay, in_chip)
        wt, wxt, gaint = call(k_top_faces, [(4, 8), (9,), (8,)], ct, edge)
        (rm,) = call(k_mid_left, [(8,)], wm, wxm, diagm, gainm, bm, m1, z, near, info=info)
        rms = gather(rm, twins)
        bt, t0, pay, ipay = call(k_top_start, [(8,), (8,), (1,), (1,)], gaint, rms)
        z = send(t0, later2)
        edge = send(pay, outer)
        near = gather(ipay, in_chip)
        mine, other = call(
            k_top, [(8,), (8,)], wt, wxt, gaint, bt, t0, edge, z, near, m1, e1, info=info
        )
        got = send(other, pair)
        (new,) = call(k_state_out, [(16,)], u_in, mine, got, info=info)
        return new[None, None], residual[None, None]

    spec = P("tm", "space", None, None, None)
    return jax.shard_map(
        shards,
        mesh=mesh,
        in_specs=(spec, spec, P("space", None, None, None)),
        out_specs=(spec, spec),
        check_vma=False,
    )
```

```python
import functools
import jax
import jax.numpy as jnp
from jax import lax
from jax.experimental import pallas as pl
from jax.experimental.pallas import tpu as pltpu
from jax.sharding import PartitionSpec as P

tau = 0.08
omega = 0.7
keep = 1.0 - omega


def routes(chips, slabs):
    def device(z, core, slab):
        return (2 * z + core) * slabs + slab

    every = [(z, c, s) for z in range(chips) for c in range(2) for s in range(slabs)]
    pair = [(device(z, c, s), device(z, 1 - c, s)) for z, c, s in every]
    outer = []
    for z, c, s in every:
        near = s - 1 if c == 0 else s + 1
        if 0 <= near < slabs:
            outer.append((device(z, c, s), device(z, 1 - c, near)))
    later = [(device(z, c, s), device(z + 1, c, s)) for z, c, s in every if z + 1 < chips]
    later2 = [(device(z, c, s), device(z + 2, c, s)) for z, c, s in every if z + 2 < chips]
    twin = [(device(z, c, s), device(z ^ 1, c, s)) for z, c, s in every]
    in_chip = [[device(z, 0, s), device(z, 1, s)] for z in range(chips) for s in range(slabs)]
    twins = [
        [device(2 * k, c, s), device(2 * k + 1, c, s)]
        for k in range(chips // 2)
        for c in range(2)
        for s in range(slabs)
    ]
    return pair, outer, later, later2, twin, in_chip, twins


def own_core():
    return lax.rem(lax.axis_index("tm"), 2)


def has_outer():
    slab = lax.axis_index("space")
    last = lax.axis_size("space") - 1
    return slab != jnp.where(own_core() == 0, 0, last)


def iota(v, axis):
    return lax.broadcasted_iota(jnp.int32, v.shape, axis)


def around(v):
    ny = v.shape[1]
    nz = v.shape[0]
    return (
        pltpu.roll(v, 1, 1),
        pltpu.roll(v, ny - 1, 1),
        pltpu.roll(v, 1, 0),
        pltpu.roll(v, nz - 1, 0),
    )


def faces(c, low, high, step):
    ny = c.shape[1]
    nz = c.shape[0]
    y = iota(c, 1)
    z = iota(c, 0)
    inside = (y > 0, y < ny - 1, z > 0, z < nz - 1)
    near = [jnp.where(ok, n, 0.0) for ok, n in zip(inside, around(c))]
    total = low + high
    for n in near:
        total = total + n
    diag = 1.0 + step * (3.0 * c + 0.5 * total)
    weights = [jnp.where(ok, (0.5 * step) * (c + n), 0.0) for ok, n in zip(inside, near)]
    return weights, (0.5 * step) * (c + high), diag


def spread(v, low, high, weights, w_low, w_high):
    flux = w_low * low + w_high * high
    for w, n in zip(weights, around(v)):
        flux = flux + w * n
    return flux


def each_row(fill):
    def rows(mirror):
        for x in range(16):
            fill(x, 15 - x if mirror else x)

    pl.when(own_core() == 0)(lambda: rows(False))
    pl.when(own_core() == 1)(lambda: rows(True))


def k_load_u(u, uo, send):
    def fill(x, row):
        if row <= 8:
            uo[row] = u[:, x, :]
        if row >= 7:
            send[15 - row] = u[:, x, :]

    each_row(fill)


def k_load_f(f, send0, fo, send):
    def fill(x, row):
        if row <= 7:
            fo[row] = f[:, x, :]
        else:
            send[24 - row] = f[:, x, :]

    each_row(fill)


def k_load_k(kap, ko):
    def fill(x, row):
        if row <= 8:
            ko[row] = kap[:, x, :]

    each_row(fill)


def k_pack(uo, fo, ko, got, u, f, edge, zu):
    h = own_core()
    for x in range(9):
        u[h, x] = uo[x]
        u[1 - h, x] = got[x]
    for x in range(8):
        f[h, x] = fo[x]
        f[1 - h, x] = got[9 + x]
        zu[x] = u[1, x]
    for x in range(3):
        edge[x] = u[0, x]
        edge[3 + x] = u[1, x]
        edge[6 + x] = ko[x]
    for x in range(2):
        edge[9 + x] = f[0, x]
        edge[11 + x] = f[1, x]


def k_inner(u, f, ko, w, wx, diag, gain, b, e0, cm, c):
    for x in range(9):
        for t in range(2):
            v = u[t, x]
            c[t, x] = ko[x] * (1.0 + v * v)
        cm[x + 3] = 0.5 * (c[0, x] + c[1, x])
    for t in range(2):
        wx[t, 3] = (0.5 * tau) * (c[t, 0] + c[t, 1])
        for x in range(1, 8):
            i = x + 2
            weights, w_high, d = faces(c[t, x], c[t, x - 1], c[t, x + 1], tau)
            wx[t, i + 1] = w_high
            for k in range(4):
                w[k, t, i] = weights[k]
            g = omega / d
            diag[t, i] = d
            gain[t, i] = g
            v = u[t, x]
            flux = spread(v, u[t, x - 1], u[t, x + 1], weights, wx[t, i], w_high)
            value = f[t, x] - d * v + flux
            if t == 1:
                value = value + u[0, x]
                e0[t, i] = g * value
            b[t, i] = value


def k_edge(
    u, f, ko, edge, w0, wx0, diag0, gain0, b0, e00, cm0, w, wx, diag, gain, b, e0, cm, zpay, c
):
    real = has_outer()

    def uu(t, x):
        return u[t, x] if x >= 0 else edge[3 * t - x - 1]

    for x in range(-3, 2):
        k = ko[x] if x >= 0 else edge[5 - x]
        for t in range(2):
            v = uu(t, x)
            c[t, x + 3] = k * (1.0 + v * v)
        if x < 0:
            cm[x + 3] = 0.5 * (c[0, x + 3] + c[1, x + 3])
    for t in range(2):
        wx[t, 0] = (0.5 * tau) * (c[t, 0] + c[t, 1])
        for x in range(-2, 1):
            i = x + 2
            weights, w_high, d = faces(c[t, i + 1], c[t, i], c[t, i + 2], tau)
            wx[t, i + 1] = w_high
            for k in range(4):
                w[k, t, i] = weights[k]
            g = omega / d
            diag[t, i] = d
            gain[t, i] = g
            v = uu(t, x)
            f_row = f[t, x] if x >= 0 else edge[8 + 2 * t - x]
            value = f_row - d * v + spread(v, uu(t, x - 1), uu(t, x + 1), weights, wx[t, i], w_high)
            if t == 1:
                value = value + uu(0, x)
            if x < 0:
                value = jnp.where(real, value, 0.0)
            b[t, i] = value
            e0[t, i] = g * value
    for i in range(9):
        zpay[i] = e0[1, i + 1]
    zpay[9] = edge[3]
    zpay[10] = edge[4]


def k_prev(zu, gain, b0, e00, b, e0, ipay):
    h = own_core()
    for x in range(8):
        value = b0[0, x + 2] + zu[x]
        b[0, x + 2] = value
        e0[0, x + 2] = gain[0, x + 2] * value
    ipay[0] = e0[0, 9]
    ipay[1] = e0[1, 9]
    for x in range(8):
        ipay[2 + x] = b[1 - h, x + 2]


def smoothed(here, low, high, w, wx, gain, t, i, right):
    weights = [w[k, t, i] for k in range(4)]
    flux = spread(here, low, high, weights, wx[t, i], wx[t, i + 1])
    return keep * here + gain[t, i] * (right + flux)


def k_fine(w, wx, gain, b, e0, near, e1, zpay):
    h = own_core()
    for t in (1, 0):
        for x in range(1 - t, 8):
            i = x + 2
            high = e0[t, i + 1] if x < 7 else near[1 - h, t]
            right = b[t, i] + e0[0, i] if t == 1 else b[t, i]
            value = smoothed(e0[t, i], e0[t, i - 1], high, w, wx, gain, t, i, right)
            e1[t, i - 1] = value
            if t == 1:
                zpay[x] = value


def k_fine_prev(w, wx, gain, b, e0, z, e10, e1, ipay):
    real = has_outer()
    for x in range(1, 8):
        i = x + 2
        e1[0, i - 1] = e10[0, i - 1] + gain[0, i] * z[i - 1]
    far, edge = [
        e0[0, i] + jnp.where(real, gain[0, i] * z[10 - i], 0.0) for i in range(2)
    ]
    e1[0, 1] = smoothed(e0[0, 2], edge, e0[0, 3], w, wx, gain, 0, 2, b[0, 2] + z[1])
    value = smoothed(edge, far, e0[0, 2], w, wx, gain, 0, 1, b[0, 1] + z[0] + z[9])
    e1[0, 0] = jnp.where(real, value, 0.0)
    value = smoothed(e0[1, 1], e0[1, 0], e0[1, 2], w, wx, gain, 1, 1, b[1, 1] + edge)
    e1[1, 0] = jnp.where(real, value, 0.0)
    ipay[0] = e1[0, 8]
    ipay[1] = e10[1, 8]


def k_mid_faces(cm, w, wx, diag, gain):
    wx[0] = tau * (cm[0] + cm[1])
    for i in range(10):
        weights, w_high, d = faces(cm[i + 1], cm[i], cm[i + 2], 2 * tau)
        wx[i + 1] = w_high
        for k in range(4):
            w[k, i] = weights[k]
        diag[i] = d
        gain[i] = omega / d


def k_restrict(w, wx, diag, b, e1, near, part):
    h = own_core()
    for x in range(8):
        i = x + 2
        value = e1[0, x + 1]
        for t in range(2):
            here = e1[t, x + 1]
            high = e1[t, x + 2] if x < 7 else near[1 - h, t]
            weights = [w[k, t, i] for k in range(4)]
            flux = spread(here, e1[t, x], high, weights, wx[t, i], wx[t, i + 1])
            value = value + (b[t, i] - diag[t, i] * here + flux)
        part[x] = value


def k_restrict_prev(part, z, gain, bm, m0, edge, ipay):
    for x in range(8):
        value = part[x] + z[x]
        bm[x] = value
        m0[x] = gain[x + 2] * value
    edge[0] = bm[0]
    edge[1] = bm[1]
    ipay[0] = m0[7]


def smoothed_mid(here, low, high, w, wx, gain, i, right):
    weights = [w[k, i] for k in range(4)]
    flux = spread(here, low, high, weights, wx[i], wx[i + 1])
    return keep * here + gain[i] * (right + flux)


def k_mid(w, wx, gain, bm, m0, near, cm, m1, cpay):
    h = own_core()
    for x in range(10):
        cpay[x] = cm[x + 2]
    for x in range(1, 8):
        high = m0[x + 1] if x < 7 else near[1 - h, 0]
        m1[x + 1] = smoothed_mid(m0[x], m0[x - 1], high, w, wx, gain, x + 2, bm[x])


def k_mid_prev(w, wx, gain, bm, m0, edge, z, m10, m1, zpay, ipay):
    real = has_outer()
    far, near = gain[0] * edge[1], gain[1] * edge[0]
    for x in range(1, 8):
        value = m10[x + 1] + gain[x + 2] * z[x]
        m1[x + 1] = value
        zpay[x] = value
    value = smoothed_mid(m0[0], near, m0[1], w, wx, gain, 2, bm[0] + z[0])
    m1[1] = value
    zpay[0] = value
    value = smoothed_mid(near, far, m0[0], w, wx, gain, 1, edge[0])
    m1[0] = jnp.where(real, value, 0.0)
    zpay[8] = near
    ipay[0] = m1[8]


def left_mid(here, low, high, w, wx, diag, i, right):
    weights = [w[k, i] for k in range(4)]
    flux = spread(here, low, high, weights, wx[i], wx[i + 1])
    return right - diag[i] * here + flux


def k_mid_left(w, wx, diag, bm, m1, near, rm):
    h = own_core()
    for x in range(1, 8):
        high = m1[x + 2] if x < 7 else near[1 - h, 0]
        rm[x] = left_mid(m1[x + 1], m1[x], high, w, wx, diag, x + 2, bm[x])


def k_mid_left_prev(w, wx, diag, gain, bm, m1, z, rm0, rm):
    real = has_outer()
    low = m1[0] + jnp.where(real, gain[1] * z[8], 0.0)
    rm[0] = left_mid(m1[1], low, m1[2], w, wx, diag, 2, bm[0] + z[0])
    for x in range(1, 8):
        rm[x] = rm0[x] + z[x]


def k_top_faces(cm, twin, _, w, wx, gain, ct):
    for i in range(10):
        ct[i] = 0.5 * (cm[i + 2] + twin[i])
    wx[0] = (2 * tau) * (ct[0] + ct[1])
    for x in range(8):
        weights, w_high, d = faces(ct[x + 1], ct[x], ct[x + 2], 4 * tau)
        wx[x + 1] = w_high
        for k in range(4):
            w[k, x] = weights[k]
        gain[x] = omega / d


def k_top_start(gain, rm, bt, t0, edge, ipay):
    for x in range(8):
        value = rm[0, x] + rm[1, x]
        bt[x] = value
        t0[x] = gain[x] * value
    edge[0] = t0[0]
    ipay[0] = t0[7]


def k_top(w, wx, gain, bt, t0, near, m1, e1, mine, other):
    h = own_core()
    for x in range(1, 8):
        high = t0[x + 1] if x < 7 else near[1 - h, 0]
        value = smoothed_mid(t0[x], t0[x - 1], high, w, wx, gain, x, bt[x]) + m1[x + 1]
        mine[x] = e1[h, x + 1] + value
        other[x] = e1[1 - h, x + 1] + value


def k_top_prev(w, wx, gain, bt, t0, edge, z, m1, e1, mine0, other0, mine, other):
    h = own_core()
    for x in range(1, 8):
        value = gain[x] * z[x]
        mine[x] = mine0[x] + value
        other[x] = other0[x] + value
    value = smoothed_mid(t0[0], edge[0], t0[1], w, wx, gain, 0, bt[0] + z[0]) + m1[1]
    mine[0] = e1[h, 1] + value
    other[0] = e1[1 - h, 1] + value


def k_residual_out(b, near, out):
    h = own_core()

    def rows(mirror):
        for x in range(16):
            row = 15 - x if mirror else x
            out[:, x, :] = b[h, row + 2] if row < 8 else near[1 - h, 2 + 15 - row]

    pl.when(h == 0)(lambda: rows(False))
    pl.when(h == 1)(lambda: rows(True))


def store_half(u, add, out, buf, sems, start, row_of):
    copies = []
    for j in range(2):
        part = pl.ds(8 * j, 8)
        for x in range(8):
            buf[part, x, :] = u[part, start + x, :] + add[row_of(x), part, :]
        copies.append(
            pltpu.make_async_copy(buf.at[part], out.at[part, pl.ds(start, 8)], sems.at[j])
        )
        copies[-1].start()
    for copy in copies:
        copy.wait()


def k_state_own(u, mine, out, buf, sems):
    pl.when(own_core() == 0)(lambda: store_half(u, mine, out, buf, sems, 0, lambda x: x))
    pl.when(own_core() == 1)(lambda: store_half(u, mine, out, buf, sems, 8, lambda x: 7 - x))


def k_state_far(u, got, out0, out, buf, sems):
    pl.when(own_core() == 0)(lambda: store_half(u, got, out, buf, sems, 8, lambda x: 7 - x))
    pl.when(own_core() == 1)(lambda: store_half(u, got, out, buf, sems, 0, lambda x: x))


VMEM = pl.BlockSpec(memory_space=pltpu.VMEM)
HBM = pl.BlockSpec(memory_space=pltpu.HBM)


def solution(mesh):
    slabs = mesh.shape["space"]
    chips = mesh.shape["tm"] // 2
    pair, outer, later, later2, twin, in_chip, twins = routes(chips, slabs)
    axes = ("tm", "space")

    def send(x, route):
        return lax.ppermute(x, axes, route)

    def gather(x, groups):
        return lax.all_gather(x, axes, axis_index_groups=groups)

    def call(kernel, shapes, *args, scratch=(), alias=(), work=20, sems=0, far=(), far_out=()):
        size = sum(a.size for a in args) * 4
        scratches = [pltpu.VMEM(s + (16, 512), jnp.float32) for s in scratch]
        if sems:
            scratches.append(pltpu.SemaphoreType.DMA((sems,)))
        return pl.pallas_call(
            kernel,
            out_shape=[jax.ShapeDtypeStruct(s + (16, 512), jnp.float32) for s in shapes],
            in_specs=[HBM if i in far else VMEM for i in range(len(args))],
            out_specs=[HBM if i in far_out else VMEM for i in range(len(shapes))],
            scratch_shapes=scratches,
            input_output_aliases=dict(alias),
            cost_estimate=pl.CostEstimate(flops=work * 131072, bytes_accessed=size, transcendentals=0),
            compiler_params=pltpu.CompilerParams(vmem_limit_bytes=24 * 2**20),
            name=kernel.__name__,
        )(*args)

    def shards(iterate, source_term, conductivity):
        u_in = iterate[0, 0]

        uo, pay = call(k_load_u, [(9,), (17,)], u_in)
        fo, pay = call(k_load_f, [(8,), (17,)], source_term[0, 0], pay, alias=[(1, 1)])
        (ko,) = call(k_load_k, [(9,)], conductivity[0])
        got = send(pay, pair)
        u, f, edge, zu = call(k_pack, [(2, 9), (2, 8), (13,), (8,)], uo, fo, ko, got)
        edge = send(edge, outer)
        zu = send(zu, later)
        fields = [(4, 2, 10), (2, 11), (2, 10), (2, 10), (2, 10), (2, 10), (12,)]
        held = call(k_inner, fields, u, f, ko, scratch=[(2, 9)])
        w, wx, diag, gain, b, e0, cm, zpay = call(
            k_edge, fields + [(11,)], u, f, ko, edge, *held,
            scratch=[(2, 5)], alias=[(4 + i, i) for i in range(7)],
        )
        z = send(zpay, later)
        b, e0, ipay = call(
            k_prev, [(2, 10), (2, 10), (10,)], zu, gain, b, e0, alias=[(2, 0), (3, 1)]
        )
        near_b = gather(ipay, in_chip)
        e1, zpay = call(k_fine, [(2, 9), (8,)], w, wx, gain, b, e0, near_b)
        z1 = send(zpay, later)
        e1, ipay = call(
            k_fine_prev, [(2, 9), (2,)], w, wx, gain, b, e0, z, e1, alias=[(6, 0)]
        )
        near = gather(ipay, in_chip)
        (residual,) = call(k_residual_out, [(16,)], b, near_b)
        (part,) = call(k_restrict, [(8,)], w, wx, diag, b, e1, near)
        wm, wxm, diagm, gainm = call(k_mid_faces, [(4, 10), (11,), (10,), (10,)], cm)
        bm, m0, pay, ipay = call(
            k_restrict_prev, [(8,), (8,), (2,), (1,)], part, z1, gainm
        )
        z = send(m0, later)
        edge = send(pay, outer)
        near = gather(ipay, in_chip)
        m1, pay = call(k_mid, [(9,), (10,)], wm, wxm, gainm, bm, m0, near, cm)
        cm_twin = send(pay, twin)
        m1, zpay, ipay = call(
            k_mid_prev, [(9,), (9,), (1,)], wm, wxm, gainm, bm, m0, edge, z, m1,
            alias=[(7, 0)],
        )
        z = send(zpay, later)
        near = gather(ipay, in_chip)
        wt, wxt, gaint = call(k_top_faces, [(4, 8), (9,), (8,)], cm, cm_twin, residual, scratch=[(10,)], far=(2,))
        (rm,) = call(k_mid_left, [(8,)], wm, wxm, diagm, bm, m1, near)
        (rm,) = call(
            k_mid_left_prev, [(8,)], wm, wxm, diagm, gainm, bm, m1, z, rm, alias=[(7, 0)]
        )
        rms = gather(rm, twins)
        bt, t0, pay, ipay = call(k_top_start, [(8,), (8,), (1,), (1,)], gaint, rms)
        z = send(t0, later2)
        edge = send(pay, outer)
        near = gather(ipay, in_chip)
        mine, other = call(
            k_top, [(8,), (8,)], wt, wxt, gaint, bt, t0, near, m1, e1
        )
        mine, other = call(
            k_top_prev, [(8,), (8,)], wt, wxt, gaint, bt, t0, edge, z, m1, e1, mine, other,
            alias=[(9, 0), (10, 1)],
        )
        got = send(other, pair)
        half = pltpu.VMEM((16, 8, 512), jnp.float32)
        own_spec = dict(
            out_shape=jax.ShapeDtypeStruct((16, 16, 512), jnp.float32),
            out_specs=HBM,
            scratch_shapes=[half, pltpu.SemaphoreType.DMA((2,))],
            compiler_params=pltpu.CompilerParams(vmem_limit_bytes=24 * 2**20),
        )
        new = pl.pallas_call(
            k_state_own, in_specs=[VMEM, VMEM], name="k_state_own", **own_spec
        )(u_in, mine)
        new = pl.pallas_call(
            k_state_far,
            in_specs=[VMEM, VMEM, HBM],
            input_output_aliases={2: 0},
            name="k_state_far",
            **own_spec,
        )(u_in, got, new)
        return new[None, None], residual[None, None]

    spec = P("tm", "space", None, None, None)
    return jax.shard_map(
        shards,
        mesh=mesh,
        in_specs=(spec, spec, P("space", None, None, None)),
        out_specs=(spec, spec),
        check_vma=False,
    )
```

```python
import functools
import jax
import jax.numpy as jnp
from jax import lax
from jax.experimental import pallas as pl
from jax.experimental.pallas import tpu as pltpu
from jax.sharding import PartitionSpec as P

tau = 0.08
omega = 0.7
keep = 1.0 - omega


def routes(chips, slabs):
    def device(z, core, slab):
        return (2 * z + core) * slabs + slab

    every = [(z, c, s) for z in range(chips) for c in range(2) for s in range(slabs)]
    pair = [(device(z, c, s), device(z, 1 - c, s)) for z, c, s in every]
    outer = []
    for z, c, s in every:
        near = s - 1 if c == 0 else s + 1
        if 0 <= near < slabs:
            outer.append((device(z, c, s), device(z, 1 - c, near)))
    later = [(device(z, c, s), device(z + 1, c, s)) for z, c, s in every if z + 1 < chips]
    later2 = [(device(z, c, s), device(z + 2, c, s)) for z, c, s in every if z + 2 < chips]
    twin = [(device(z, c, s), device(z ^ 1, c, s)) for z, c, s in every]
    in_chip = [[device(z, 0, s), device(z, 1, s)] for z in range(chips) for s in range(slabs)]
    twins = [
        [device(2 * k, c, s), device(2 * k + 1, c, s)]
        for k in range(chips // 2)
        for c in range(2)
        for s in range(slabs)
    ]
    return pair, outer, later, later2, twin, in_chip, twins


def own_core():
    return lax.rem(lax.axis_index("tm"), 2)


def has_outer():
    slab = lax.axis_index("space")
    last = lax.axis_size("space") - 1
    return slab != jnp.where(own_core() == 0, 0, last)


def iota(v, axis):
    return lax.broadcasted_iota(jnp.int32, v.shape, axis)


def around(v):
    ny = v.shape[1]
    nz = v.shape[0]
    return (
        pltpu.roll(v, 1, 1),
        pltpu.roll(v, ny - 1, 1),
        pltpu.roll(v, 1, 0),
        pltpu.roll(v, nz - 1, 0),
    )


def faces(c, low, high, step):
    ny = c.shape[1]
    nz = c.shape[0]
    y = iota(c, 1)
    z = iota(c, 0)
    inside = (y > 0, y < ny - 1, z > 0, z < nz - 1)
    near = [jnp.where(ok, n, 0.0) for ok, n in zip(inside, around(c))]
    total = low + high
    for n in near:
        total = total + n
    diag = 1.0 + step * (3.0 * c + 0.5 * total)
    weights = [jnp.where(ok, (0.5 * step) * (c + n), 0.0) for ok, n in zip(inside, near)]
    return weights, (0.5 * step) * (c + high), diag


def spread(v, low, high, weights, w_low, w_high):
    flux = w_low * low + w_high * high
    for w, n in zip(weights, around(v)):
        flux = flux + w * n
    return flux


def each_row(fill):
    def rows(mirror):
        for x in range(16):
            fill(x, 15 - x if mirror else x)

    pl.when(own_core() == 0)(lambda: rows(False))
    pl.when(own_core() == 1)(lambda: rows(True))


def k_load_u(u, uo, send):
    def fill(x, row):
        if row <= 10:
            uo[row] = u[:, x, :]
        if row >= 5:
            send[15 - row] = u[:, x, :]

    each_row(fill)


def k_load_f(f, send0, fo, send):
    def fill(x, row):
        if row <= 9:
            fo[row] = f[:, x, :]
        if row >= 6:
            send[26 - row] = f[:, x, :]

    each_row(fill)


def k_load_k(kap, ko):
    def fill(x, row):
        if row <= 10:
            ko[row] = kap[:, x, :]

    each_row(fill)


def k_pack(uo, fo, ko, got, u, f, edge, zu):
    h = own_core()
    for x in range(11):
        u[h, x] = uo[x]
        u[1 - h, x] = got[x]
    for x in range(10):
        f[h, x] = fo[x]
        f[1 - h, x] = got[11 + x]
        zu[x] = u[1, x]
    for x in range(3):
        edge[x] = u[0, x]
        edge[3 + x] = u[1, x]
        edge[6 + x] = ko[x]
    for x in range(2):
        edge[9 + x] = f[0, x]
        edge[11 + x] = f[1, x]


def k_inner(u, f, ko, w, wx, diag, gain, b, e0, cm, c):
    for x in range(11):
        for t in range(2):
            v = u[t, x]
            c[t, x] = ko[x] * (1.0 + v * v)
        if x < 9:
            cm[x + 3] = 0.5 * (c[0, x] + c[1, x])
    for t in range(2):
        wx[t, 3] = (0.5 * tau) * (c[t, 0] + c[t, 1])
        for x in range(1, 10):
            i = x + 2
            weights, w_high, d = faces(c[t, x], c[t, x - 1], c[t, x + 1], tau)
            wx[t, i + 1] = w_high
            for k in range(4):
                w[k, t, i] = weights[k]
            g = omega / d
            diag[t, i] = d
            gain[t, i] = g
            v = u[t, x]
            flux = spread(v, u[t, x - 1], u[t, x + 1], weights, wx[t, i], w_high)
            value = f[t, x] - d * v + flux
            if t == 1:
                value = value + u[0, x]
                e0[t, i] = g * value
            b[t, i] = value


def k_edge(
    u, f, ko, edge, w0, wx0, diag0, gain0, b0, e00, cm0, w, wx, diag, gain, b, e0, cm, zpay, c
):
    real = has_outer()

    def uu(t, x):
        return u[t, x] if x >= 0 else edge[3 * t - x - 1]

    for x in range(-3, 2):
        k = ko[x] if x >= 0 else edge[5 - x]
        for t in range(2):
            v = uu(t, x)
            c[t, x + 3] = k * (1.0 + v * v)
        if x < 0:
            cm[x + 3] = 0.5 * (c[0, x + 3] + c[1, x + 3])
    for t in range(2):
        wx[t, 0] = (0.5 * tau) * (c[t, 0] + c[t, 1])
        for x in range(-2, 1):
            i = x + 2
            weights, w_high, d = faces(c[t, i + 1], c[t, i], c[t, i + 2], tau)
            wx[t, i + 1] = w_high
            for k in range(4):
                w[k, t, i] = weights[k]
            g = omega / d
            diag[t, i] = d
            gain[t, i] = g
            v = uu(t, x)
            f_row = f[t, x] if x >= 0 else edge[8 + 2 * t - x]
            value = f_row - d * v + spread(v, uu(t, x - 1), uu(t, x + 1), weights, wx[t, i], w_high)
            if t == 1:
                value = value + uu(0, x)
            if x < 0:
                value = jnp.where(real, value, 0.0)
            b[t, i] = value
            e0[t, i] = g * value
    for i in range(10):
        zpay[i] = e0[1, i + 1]
    zpay[10] = edge[3]
    zpay[11] = edge[4]


def k_prev(zu, gain, b0, e00, b, e0):
    for x in range(10):
        value = b0[0, x + 2] + zu[x]
        b[0, x + 2] = value
        e0[0, x + 2] = gain[0, x + 2] * value


def smoothed(here, low, high, w, wx, gain, t, i, right):
    weights = [w[k, t, i] for k in range(4)]
    flux = spread(here, low, high, weights, wx[t, i], wx[t, i + 1])
    return keep * here + gain[t, i] * (right + flux)


def k_fine(w, wx, gain, b, e0, e1, zpay):
    for t in (1, 0):
        for x in range(1 - t, 9):
            i = x + 2
            right = b[t, i] + e0[0, i] if t == 1 else b[t, i]
            value = smoothed(e0[t, i], e0[t, i - 1], e0[t, i + 1], w, wx, gain, t, i, right)
            e1[t, i - 1] = value
            if t == 1 and x < 8:
                zpay[x] = value


def k_fine_prev(w, wx, gain, b, e0, z, e10, e1):
    real = has_outer()
    for x in range(1, 9):
        i = x + 2
        e1[0, i - 1] = e10[0, i - 1] + gain[0, i] * z[i - 1]
    far, edge = [
        e0[0, i] + jnp.where(real, gain[0, i] * z[11 - i], 0.0) for i in range(2)
    ]
    e1[0, 1] = smoothed(e0[0, 2], edge, e0[0, 3], w, wx, gain, 0, 2, b[0, 2] + z[1])
    value = smoothed(edge, far, e0[0, 2], w, wx, gain, 0, 1, b[0, 1] + z[0] + z[10])
    e1[0, 0] = jnp.where(real, value, 0.0)
    value = smoothed(e0[1, 1], e0[1, 0], e0[1, 2], w, wx, gain, 1, 1, b[1, 1] + edge)
    e1[1, 0] = jnp.where(real, value, 0.0)


def k_mid_faces(cm, w, wx, diag, gain):
    wx[0] = tau * (cm[0] + cm[1])
    for i in range(10):
        weights, w_high, d = faces(cm[i + 1], cm[i], cm[i + 2], 2 * tau)
        wx[i + 1] = w_high
        for k in range(4):
            w[k, i] = weights[k]
        diag[i] = d
        gain[i] = omega / d


def k_restrict(w, wx, diag, b, e1, cm, part, cpay):
    for x in range(8):
        i = x + 2
        value = e1[0, x + 1]
        for t in range(2):
            here = e1[t, x + 1]
            weights = [w[k, t, i] for k in range(4)]
            flux = spread(here, e1[t, x], e1[t, x + 2], weights, wx[t, i], wx[t, i + 1])
            value = value + (b[t, i] - diag[t, i] * here + flux)
        part[x] = value
    for x in range(10):
        cpay[x] = cm[x + 2]


def k_restrict_prev(part, z, gain, b, bm, m0, edge, ipay):
    h = own_core()
    for x in range(8):
        value = part[x] + z[x]
        bm[x] = value
        m0[x] = gain[x + 2] * value
        ipay[1 + x] = b[1 - h, x + 2]
    edge[0] = bm[0]
    edge[1] = bm[1]
    ipay[0] = m0[7]


def smoothed_mid(here, low, high, w, wx, gain, i, right):
    weights = [w[k, i] for k in range(4)]
    flux = spread(here, low, high, weights, wx[i], wx[i + 1])
    return keep * here + gain[i] * (right + flux)


def k_mid(w, wx, gain, bm, m0, near, _, m1):
    h = own_core()
    for x in range(1, 8):
        high = m0[x + 1] if x < 7 else near[1 - h, 0]
        m1[x + 1] = smoothed_mid(m0[x], m0[x - 1], high, w, wx, gain, x + 2, bm[x])


def k_mid_prev(w, wx, gain, bm, m0, edge, z, m10, m1, zpay, ipay):
    real = has_outer()
    far, near = gain[0] * edge[1], gain[1] * edge[0]
    for x in range(1, 8):
        value = m10[x + 1] + gain[x + 2] * z[x]
        m1[x + 1] = value
        zpay[x] = value
    value = smoothed_mid(m0[0], near, m0[1], w, wx, gain, 2, bm[0] + z[0])
    m1[1] = value
    zpay[0] = value
    value = smoothed_mid(near, far, m0[0], w, wx, gain, 1, edge[0])
    m1[0] = jnp.where(real, value, 0.0)
    zpay[8] = near
    ipay[0] = m1[8]


def left_mid(here, low, high, w, wx, diag, i, right):
    weights = [w[k, i] for k in range(4)]
    flux = spread(here, low, high, weights, wx[i], wx[i + 1])
    return right - diag[i] * here + flux


def k_mid_left(w, wx, diag, bm, m1, near, rm):
    h = own_core()
    for x in range(1, 8):
        high = m1[x + 2] if x < 7 else near[1 - h, 0]
        rm[x] = left_mid(m1[x + 1], m1[x], high, w, wx, diag, x + 2, bm[x])


def k_mid_left_prev(w, wx, diag, gain, bm, m1, z, rm0, rm):
    real = has_outer()
    low = m1[0] + jnp.where(real, gain[1] * z[8], 0.0)
    rm[0] = left_mid(m1[1], low, m1[2], w, wx, diag, 2, bm[0] + z[0])
    for x in range(1, 8):
        rm[x] = rm0[x] + z[x]


def k_top_faces(ct, w, wx, gain):
    wx[0] = (2 * tau) * (ct[0] + ct[1])
    for x in range(8):
        weights, w_high, d = faces(ct[x + 1], ct[x], ct[x + 2], 4 * tau)
        wx[x + 1] = w_high
        for k in range(4):
            w[k, x] = weights[k]
        gain[x] = omega / d


def k_top_start(gain, rm, bt, t0, edge, ipay):
    for x in range(8):
        value = rm[0, x] + rm[1, x]
        bt[x] = value
        t0[x] = gain[x] * value
    edge[0] = t0[0]
    ipay[0] = t0[7]


def k_top(w, wx, gain, bt, t0, near, m1, e1, mine, other):
    h = own_core()
    for x in range(1, 8):
        high = t0[x + 1] if x < 7 else near[1 - h, 0]
        value = smoothed_mid(t0[x], t0[x - 1], high, w, wx, gain, x, bt[x]) + m1[x + 1]
        mine[x] = e1[h, x + 1] + value
        other[x] = e1[1 - h, x + 1] + value


def k_top_prev(w, wx, gain, bt, t0, edge, z, m1, e1, mine0, other0, mine, other):
    h = own_core()
    for x in range(1, 8):
        value = gain[x] * z[x]
        mine[x] = mine0[x] + value
        other[x] = other0[x] + value
    value = smoothed_mid(t0[0], edge[0], t0[1], w, wx, gain, 0, bt[0] + z[0]) + m1[1]
    mine[0] = e1[h, 1] + value
    other[0] = e1[1 - h, 1] + value


def k_residual_out(b, near, cm, twin, out, ct):
    h = own_core()
    for i in range(10):
        ct[i] = 0.5 * (cm[i + 2] + twin[i])

    def rows(mirror):
        for x in range(16):
            row = 15 - x if mirror else x
            out[:, x, :] = b[h, row + 2] if row < 8 else near[1 - h, 16 - row]

    pl.when(h == 0)(lambda: rows(False))
    pl.when(h == 1)(lambda: rows(True))


def k_state(u, mine, got, out, buf, sems):
    def store(mirror):
        far = 0 if mirror else 8
        copies = []
        for start in (8 - far, far):
            for j in range(2):
                part = pl.ds(8 * j, 8)
                for x in range(start, start + 8):
                    row = 15 - x if mirror else x
                    if row < 8:
                        add = mine[row, part, :]
                    else:
                        add = got[1 - int(mirror), 15 - row, part, :]
                    buf[part, x, :] = u[part, x, :] + add
                where = (part, pl.ds(start, 8))
                copies.append(
                    pltpu.make_async_copy(buf.at[where], out.at[where], sems.at[len(copies)])
                )
                copies[-1].start()
        for copy in copies:
            copy.wait()

    pl.when(own_core() == 0)(lambda: store(False))
    pl.when(own_core() == 1)(lambda: store(True))


VMEM = pl.BlockSpec(memory_space=pltpu.VMEM)
HBM = pl.BlockSpec(memory_space=pltpu.HBM)


def solution(mesh):
    slabs = mesh.shape["space"]
    chips = mesh.shape["tm"] // 2
    pair, outer, later, later2, twin, in_chip, twins = routes(chips, slabs)
    axes = ("tm", "space")

    def send(x, route):
        return lax.ppermute(x, axes, route)

    def gather(x, groups):
        return lax.all_gather(x, axes, axis_index_groups=groups)

    def call(kernel, shapes, *args, scratch=(), alias=(), work=20, sems=0, far=(), far_out=()):
        size = sum(a.size for a in args) * 4
        scratches = [pltpu.VMEM(s + (16, 512), jnp.float32) for s in scratch]
        if sems:
            scratches.append(pltpu.SemaphoreType.DMA((sems,)))
        return pl.pallas_call(
            kernel,
            out_shape=[jax.ShapeDtypeStruct(s + (16, 512), jnp.float32) for s in shapes],
            in_specs=[HBM if i in far else VMEM for i in range(len(args))],
            out_specs=[HBM if i in far_out else VMEM for i in range(len(shapes))],
            scratch_shapes=scratches,
            input_output_aliases=dict(alias),
            cost_estimate=pl.CostEstimate(flops=work * 131072, bytes_accessed=size, transcendentals=0),
            compiler_params=pltpu.CompilerParams(vmem_limit_bytes=24 * 2**20),
            name=kernel.__name__,
        )(*args)

    def shards(iterate, source_term, conductivity):
        u_in = iterate[0, 0]

        uo, pay = call(k_load_u, [(11,), (21,)], u_in)
        fo, pay = call(k_load_f, [(10,), (21,)], source_term[0, 0], pay, alias=[(1, 1)])
        (ko,) = call(k_load_k, [(11,)], conductivity[0])
        got = send(pay, pair)
        u, f, edge, zu = call(k_pack, [(2, 11), (2, 10), (13,), (10,)], uo, fo, ko, got)
        edge = send(edge, outer)
        zu = send(zu, later)
        fields = [(4, 2, 12), (2, 13), (2, 12), (2, 12), (2, 12), (2, 12), (12,)]
        held = call(k_inner, fields, u, f, ko, scratch=[(2, 11)])
        w, wx, diag, gain, b, e0, cm, zpay = call(
            k_edge, fields + [(12,)], u, f, ko, edge, *held,
            scratch=[(2, 5)], alias=[(4 + i, i) for i in range(7)],
        )
        z = send(zpay, later)
        b, e0 = call(k_prev, [(2, 12), (2, 12)], zu, gain, b, e0, alias=[(2, 0), (3, 1)])
        e1, zpay = call(k_fine, [(2, 10), (8,)], w, wx, gain, b, e0)
        z1 = send(zpay, later)
        (e1,) = call(k_fine_prev, [(2, 10)], w, wx, gain, b, e0, z, e1, alias=[(6, 0)])
        part, pay = call(k_restrict, [(8,), (10,)], w, wx, diag, b, e1, cm)
        cm_twin = send(pay, twin)
        wm, wxm, diagm, gainm = call(k_mid_faces, [(4, 10), (11,), (10,), (10,)], cm)
        bm, m0, pay, ipay = call(
            k_restrict_prev, [(8,), (8,), (2,), (9,)], part, z1, gainm, b
        )
        z = send(m0, later)
        edge = send(pay, outer)
        near = gather(ipay, in_chip)
        residual, ct = call(k_residual_out, [(16,), (10,)], b, near, cm, cm_twin)
        (m1,) = call(k_mid, [(9,)], wm, wxm, gainm, bm, m0, near, cm_twin, far=(6,))
        m1, zpay, ipay = call(
            k_mid_prev, [(9,), (9,), (1,)], wm, wxm, gainm, bm, m0, edge, z, m1,
            alias=[(7, 0)],
        )
        z = send(zpay, later)
        near = gather(ipay, in_chip)
        wt, wxt, gaint = call(k_top_faces, [(4, 8), (9,), (8,)], ct)
        (rm,) = call(k_mid_left, [(8,)], wm, wxm, diagm, bm, m1, near)
        (rm,) = call(
            k_mid_left_prev, [(8,)], wm, wxm, diagm, gainm, bm, m1, z, rm, alias=[(7, 0)]
        )
        rms = gather(rm, twins)
        bt, t0, pay, ipay = call(k_top_start, [(8,), (8,), (1,), (1,)], gaint, rms)
        z = send(t0, later2)
        edge = send(pay, outer)
        near = gather(ipay, in_chip)
        mine, other = call(
            k_top, [(8,), (8,)], wt, wxt, gaint, bt, t0, near, m1, e1
        )
        mine, other = call(
            k_top_prev, [(8,), (8,)], wt, wxt, gaint, bt, t0, edge, z, m1, e1, mine, other,
            alias=[(9, 0), (10, 1)],
        )
        got = gather(other, in_chip)
        new = pl.pallas_call(
            k_state,
            out_shape=jax.ShapeDtypeStruct((16, 16, 512), jnp.float32),
            in_specs=[VMEM, VMEM, VMEM],
            out_specs=HBM,
            scratch_shapes=[
                pltpu.VMEM((16, 16, 512), jnp.float32),
                pltpu.SemaphoreType.DMA((4,)),
            ],
            compiler_params=pltpu.CompilerParams(vmem_limit_bytes=24 * 2**20),
            name="k_state",
        )(u_in, mine, got)
        return new[None, None], residual[None, None]

    spec = P("tm", "space", None, None, None)
    return jax.shard_map(
        shards,
        mesh=mesh,
        in_specs=(spec, spec, P("space", None, None, None)),
        out_specs=(spec, spec),
        check_vma=False,
    )
```

```python
import functools
import jax
import jax.numpy as jnp
from jax import lax
from jax.experimental import pallas as pl
from jax.experimental.pallas import tpu as pltpu
from jax.sharding import PartitionSpec as P

tau = 0.08
omega = 0.7
keep = 1.0 - omega


def routes(chips, slabs):
    def device(z, core, slab):
        return (2 * z + core) * slabs + slab

    every = [(z, c, s) for z in range(chips) for c in range(2) for s in range(slabs)]
    pair = [(device(z, c, s), device(z, 1 - c, s)) for z, c, s in every]
    outer = []
    for z, c, s in every:
        near = s - 1 if c == 0 else s + 1
        if 0 <= near < slabs:
            outer.append((device(z, c, s), device(z, 1 - c, near)))
    later = [(device(z, c, s), device(z + 1, c, s)) for z, c, s in every if z + 1 < chips]
    later2 = [(device(z, c, s), device(z + 2, c, s)) for z, c, s in every if z + 2 < chips]
    twin = [(device(z, c, s), device(z ^ 1, c, s)) for z, c, s in every]
    in_chip = [[device(z, 0, s), device(z, 1, s)] for z in range(chips) for s in range(slabs)]
    twins = [
        [device(2 * k, c, s), device(2 * k + 1, c, s)]
        for k in range(chips // 2)
        for c in range(2)
        for s in range(slabs)
    ]
    return pair, outer, later, later2, twin, in_chip, twins


def own_core():
    return lax.rem(lax.axis_index("tm"), 2)


def has_outer():
    slab = lax.axis_index("space")
    last = lax.axis_size("space") - 1
    return slab != jnp.where(own_core() == 0, 0, last)


def iota(v, axis):
    return lax.broadcasted_iota(jnp.int32, v.shape, axis)


def around(v):
    ny = v.shape[1]
    nz = v.shape[0]
    return (
        pltpu.roll(v, 1, 1),
        pltpu.roll(v, ny - 1, 1),
        pltpu.roll(v, 1, 0),
        pltpu.roll(v, nz - 1, 0),
    )


def faces(c, low, high, step):
    ny = c.shape[1]
    nz = c.shape[0]
    y = iota(c, 1)
    z = iota(c, 0)
    inside = (y > 0, y < ny - 1, z > 0, z < nz - 1)
    near = [jnp.where(ok, n, 0.0) for ok, n in zip(inside, around(c))]
    total = low + high
    for n in near:
        total = total + n
    diag = 1.0 + step * (3.0 * c + 0.5 * total)
    weights = [jnp.where(ok, (0.5 * step) * (c + n), 0.0) for ok, n in zip(inside, near)]
    return weights, (0.5 * step) * (c + high), diag


def spread(v, low, high, weights, w_low, w_high):
    flux = w_low * low + w_high * high
    for w, n in zip(weights, around(v)):
        flux = flux + w * n
    return flux


def each_row(fill):
    def rows(mirror):
        for x in range(16):
            fill(x, 15 - x if mirror else x)

    pl.when(own_core() == 0)(lambda: rows(False))
    pl.when(own_core() == 1)(lambda: rows(True))


def k_load_u(u, uo, send):
    def fill(x, row):
        if row <= 10:
            uo[row] = u[:, x, :]
        if row >= 5:
            send[15 - row] = u[:, x, :]

    each_row(fill)


def k_load_f(f, send0, fo, send):
    def fill(x, row):
        if row <= 9:
            fo[row] = f[:, x, :]
        if row >= 6:
            send[26 - row] = f[:, x, :]

    each_row(fill)


def k_load_k(kap, ko):
    def fill(x, row):
        if row <= 10:
            ko[row] = kap[:, x, :]

    each_row(fill)


def k_pack(uo, fo, ko, got, u, f, edge, zu):
    h = own_core()
    for x in range(11):
        u[h, x] = uo[x]
        u[1 - h, x] = got[x]
    for x in range(10):
        f[h, x] = fo[x]
        f[1 - h, x] = got[11 + x]
        zu[x] = u[1, x]
    for x in range(3):
        edge[x] = u[0, x]
        edge[3 + x] = u[1, x]
        edge[6 + x] = ko[x]
    for x in range(2):
        edge[9 + x] = f[0, x]
        edge[11 + x] = f[1, x]


def k_inner(u, f, ko, w, wx, diag, gain, b, e0, cm, c):
    for x in range(11):
        for t in range(2):
            v = u[t, x]
            c[t, x] = ko[x] * (1.0 + v * v)
        if x < 9:
            cm[x + 3] = 0.5 * (c[0, x] + c[1, x])
    for t in range(2):
        wx[t, 3] = (0.5 * tau) * (c[t, 0] + c[t, 1])
        for x in range(1, 10):
            i = x + 2
            weights, w_high, d = faces(c[t, x], c[t, x - 1], c[t, x + 1], tau)
            wx[t, i + 1] = w_high
            for k in range(4):
                w[k, t, i] = weights[k]
            g = omega / d
            diag[t, i] = d
            gain[t, i] = g
            v = u[t, x]
            flux = spread(v, u[t, x - 1], u[t, x + 1], weights, wx[t, i], w_high)
            value = f[t, x] - d * v + flux
            if t == 1:
                value = value + u[0, x]
                e0[t, i] = g * value
            b[t, i] = value


def k_edge(
    u, f, ko, edge, w0, wx0, diag0, gain0, b0, e00, cm0, w, wx, diag, gain, b, e0, cm, zpay, c
):
    real = has_outer()

    def uu(t, x):
        return u[t, x] if x >= 0 else edge[3 * t - x - 1]

    for x in range(-3, 2):
        k = ko[x] if x >= 0 else edge[5 - x]
        for t in range(2):
            v = uu(t, x)
            c[t, x + 3] = k * (1.0 + v * v)
        if x < 0:
            cm[x + 3] = 0.5 * (c[0, x + 3] + c[1, x + 3])
    for t in range(2):
        wx[t, 0] = (0.5 * tau) * (c[t, 0] + c[t, 1])
        for x in range(-2, 1):
            i = x + 2
            weights, w_high, d = faces(c[t, i + 1], c[t, i], c[t, i + 2], tau)
            wx[t, i + 1] = w_high
            for k in range(4):
                w[k, t, i] = weights[k]
            g = omega / d
            diag[t, i] = d
            gain[t, i] = g
            v = uu(t, x)
            f_row = f[t, x] if x >= 0 else edge[8 + 2 * t - x]
            value = f_row - d * v + spread(v, uu(t, x - 1), uu(t, x + 1), weights, wx[t, i], w_high)
            if t == 1:
                value = value + uu(0, x)
            if x < 0:
                value = jnp.where(real, value, 0.0)
            b[t, i] = value
            e0[t, i] = g * value
    for i in range(10):
        zpay[i] = e0[1, i + 1]
    zpay[10] = edge[3]
    zpay[11] = edge[4]


def k_prev(zu, gain, b0, e00, b, e0):
    for x in range(10):
        value = b0[0, x + 2] + zu[x]
        b[0, x + 2] = value
        e0[0, x + 2] = gain[0, x + 2] * value


def smoothed(here, low, high, w, wx, gain, t, i, right):
    weights = [w[k, t, i] for k in range(4)]
    flux = spread(here, low, high, weights, wx[t, i], wx[t, i + 1])
    return keep * here + gain[t, i] * (right + flux)


def k_fine(w, wx, gain, b, e0, e1, zpay):
    for t in (1, 0):
        for x in range(1 - t, 9):
            i = x + 2
            right = b[t, i] + e0[0, i] if t == 1 else b[t, i]
            value = smoothed(e0[t, i], e0[t, i - 1], e0[t, i + 1], w, wx, gain, t, i, right)
            e1[t, i - 1] = value
            if t == 1 and x < 8:
                zpay[x] = value


def k_fine_prev(w, wx, gain, b, e0, z, e10, e1):
    real = has_outer()
    for x in range(1, 9):
        i = x + 2
        e1[0, i - 1] = e10[0, i - 1] + gain[0, i] * z[i - 1]
    far, edge = [
        e0[0, i] + jnp.where(real, gain[0, i] * z[11 - i], 0.0) for i in range(2)
    ]
    e1[0, 1] = smoothed(e0[0, 2], edge, e0[0, 3], w, wx, gain, 0, 2, b[0, 2] + z[1])
    value = smoothed(edge, far, e0[0, 2], w, wx, gain, 0, 1, b[0, 1] + z[0] + z[10])
    e1[0, 0] = jnp.where(real, value, 0.0)
    value = smoothed(e0[1, 1], e0[1, 0], e0[1, 2], w, wx, gain, 1, 1, b[1, 1] + edge)
    e1[1, 0] = jnp.where(real, value, 0.0)


def k_mid_faces(cm, w, wx, diag, gain):
    wx[0] = tau * (cm[0] + cm[1])
    for i in range(10):
        weights, w_high, d = faces(cm[i + 1], cm[i], cm[i + 2], 2 * tau)
        wx[i + 1] = w_high
        for k in range(4):
            w[k, i] = weights[k]
        diag[i] = d
        gain[i] = omega / d


def k_restrict(w, wx, diag, b, e1, cm, part, cpay):
    for x in range(8):
        i = x + 2
        value = e1[0, x + 1]
        for t in range(2):
            here = e1[t, x + 1]
            weights = [w[k, t, i] for k in range(4)]
            flux = spread(here, e1[t, x], e1[t, x + 2], weights, wx[t, i], wx[t, i + 1])
            value = value + (b[t, i] - diag[t, i] * here + flux)
        part[x] = value
    for x in range(10):
        cpay[x] = cm[x + 2]


def k_restrict_prev(part, z, gain, bm, m0, edge, ipay):
    for x in range(8):
        value = part[x] + z[x]
        bm[x] = value
        m0[x] = gain[x + 2] * value
    edge[0] = bm[0]
    edge[1] = bm[1]
    ipay[0] = m0[7]


def smoothed_mid(here, low, high, w, wx, gain, i, right):
    weights = [w[k, i] for k in range(4)]
    flux = spread(here, low, high, weights, wx[i], wx[i + 1])
    return keep * here + gain[i] * (right + flux)


def k_mid(w, wx, gain, bm, m0, near, _, m1):
    h = own_core()
    for x in range(1, 8):
        high = m0[x + 1] if x < 7 else near[1 - h, 0]
        m1[x + 1] = smoothed_mid(m0[x], m0[x - 1], high, w, wx, gain, x + 2, bm[x])


def k_mid_prev(w, wx, gain, bm, m0, edge, z, m10, b, m1, zpay, ipay):
    h = own_core()
    for x in range(8):
        ipay[1 + x] = b[1 - h, x + 2]
    real = has_outer()
    far, near = gain[0] * edge[1], gain[1] * edge[0]
    for x in range(1, 8):
        value = m10[x + 1] + gain[x + 2] * z[x]
        m1[x + 1] = value
        zpay[x] = value
    value = smoothed_mid(m0[0], near, m0[1], w, wx, gain, 2, bm[0] + z[0])
    m1[1] = value
    zpay[0] = value
    value = smoothed_mid(near, far, m0[0], w, wx, gain, 1, edge[0])
    m1[0] = jnp.where(real, value, 0.0)
    zpay[8] = near
    ipay[0] = m1[8]


def left_mid(here, low, high, w, wx, diag, i, right):
    weights = [w[k, i] for k in range(4)]
    flux = spread(here, low, high, weights, wx[i], wx[i + 1])
    return right - diag[i] * here + flux


def k_mid_left(w, wx, diag, bm, m1, near, rm):
    h = own_core()
    for x in range(1, 8):
        high = m1[x + 2] if x < 7 else near[1 - h, 0]
        rm[x] = left_mid(m1[x + 1], m1[x], high, w, wx, diag, x + 2, bm[x])


def k_mid_left_prev(w, wx, diag, gain, bm, m1, z, rm0, rm):
    real = has_outer()
    low = m1[0] + jnp.where(real, gain[1] * z[8], 0.0)
    rm[0] = left_mid(m1[1], low, m1[2], w, wx, diag, 2, bm[0] + z[0])
    for x in range(1, 8):
        rm[x] = rm0[x] + z[x]


def k_top_faces(ct, w, wx, gain):
    wx[0] = (2 * tau) * (ct[0] + ct[1])
    for x in range(8):
        weights, w_high, d = faces(ct[x + 1], ct[x], ct[x + 2], 4 * tau)
        wx[x + 1] = w_high
        for k in range(4):
            w[k, x] = weights[k]
        gain[x] = omega / d


def k_top_start(gain, rm, bt, t0, edge, ipay):
    for x in range(8):
        value = rm[0, x] + rm[1, x]
        bt[x] = value
        t0[x] = gain[x] * value
    edge[0] = t0[0]
    ipay[0] = t0[7]


def k_top(w, wx, gain, bt, t0, near, m1, e1, mine, other):
    h = own_core()
    for x in range(1, 8):
        high = t0[x + 1] if x < 7 else near[1 - h, 0]
        value = smoothed_mid(t0[x], t0[x - 1], high, w, wx, gain, x, bt[x]) + m1[x + 1]
        mine[x] = e1[h, x + 1] + value
        other[x] = e1[1 - h, x + 1] + value


def k_top_prev(w, wx, gain, bt, t0, edge, z, m1, e1, mine0, other0, mine, other):
    h = own_core()
    for x in range(1, 8):
        value = gain[x] * z[x]
        mine[x] = mine0[x] + value
        other[x] = other0[x] + value
    value = smoothed_mid(t0[0], edge[0], t0[1], w, wx, gain, 0, bt[0] + z[0]) + m1[1]
    mine[0] = e1[h, 1] + value
    other[0] = e1[1 - h, 1] + value


def k_residual_out(b, near, cm, twin, out, ct):
    h = own_core()
    for i in range(10):
        ct[i] = 0.5 * (cm[i + 2] + twin[i])

    def rows(mirror):
        for x in range(16):
            row = 15 - x if mirror else x
            out[:, x, :] = b[h, row + 2] if row < 8 else near[1 - h, 16 - row]

    pl.when(h == 0)(lambda: rows(False))
    pl.when(h == 1)(lambda: rows(True))


def k_state(u, mine, got, out, buf, sems):
    def store(mirror):
        far = 0 if mirror else 8
        copies = []
        for start in (8 - far, far):
            for j in range(2):
                part = pl.ds(8 * j, 8)
                for x in range(start, start + 8):
                    row = 15 - x if mirror else x
                    if row < 8:
                        add = mine[row, part, :]
                    else:
                        add = got[1 - int(mirror), 15 - row, part, :]
                    buf[part, x, :] = u[part, x, :] + add
                where = (part, pl.ds(start, 8))
                copies.append(
                    pltpu.make_async_copy(buf.at[where], out.at[where], sems.at[len(copies)])
                )
                copies[-1].start()
        for copy in copies:
            copy.wait()

    pl.when(own_core() == 0)(lambda: store(False))
    pl.when(own_core() == 1)(lambda: store(True))


VMEM = pl.BlockSpec(memory_space=pltpu.VMEM)
HBM = pl.BlockSpec(memory_space=pltpu.HBM)


def solution(mesh):
    slabs = mesh.shape["space"]
    chips = mesh.shape["tm"] // 2
    pair, outer, later, later2, twin, in_chip, twins = routes(chips, slabs)
    axes = ("tm", "space")

    def send(x, route):
        return lax.ppermute(x, axes, route)

    def gather(x, groups):
        return lax.all_gather(x, axes, axis_index_groups=groups)

    def call(kernel, shapes, *args, scratch=(), alias=(), work=20, sems=0, far=(), far_out=()):
        size = sum(a.size for a in args) * 4
        scratches = [pltpu.VMEM(s + (16, 512), jnp.float32) for s in scratch]
        if sems:
            scratches.append(pltpu.SemaphoreType.DMA((sems,)))
        return pl.pallas_call(
            kernel,
            out_shape=[jax.ShapeDtypeStruct(s + (16, 512), jnp.float32) for s in shapes],
            in_specs=[HBM if i in far else VMEM for i in range(len(args))],
            out_specs=[HBM if i in far_out else VMEM for i in range(len(shapes))],
            scratch_shapes=scratches,
            input_output_aliases=dict(alias),
            cost_estimate=pl.CostEstimate(flops=work * 131072, bytes_accessed=size, transcendentals=0),
            compiler_params=pltpu.CompilerParams(vmem_limit_bytes=24 * 2**20),
            name=kernel.__name__,
        )(*args)

    def shards(iterate, source_term, conductivity):
        u_in = iterate[0, 0]

        uo, pay = call(k_load_u, [(11,), (21,)], u_in)
        fo, pay = call(k_load_f, [(10,), (21,)], source_term[0, 0], pay, alias=[(1, 1)])
        (ko,) = call(k_load_k, [(11,)], conductivity[0])
        got = send(pay, pair)
        u, f, edge, zu = call(k_pack, [(2, 11), (2, 10), (13,), (10,)], uo, fo, ko, got)
        edge = send(edge, outer)
        zu = send(zu, later)
        fields = [(4, 2, 12), (2, 13), (2, 12), (2, 12), (2, 12), (2, 12), (12,)]
        held = call(k_inner, fields, u, f, ko, scratch=[(2, 11)])
        w, wx, diag, gain, b, e0, cm, zpay = call(
            k_edge, fields + [(12,)], u, f, ko, edge, *held,
            scratch=[(2, 5)], alias=[(4 + i, i) for i in range(7)],
        )
        z = send(zpay, later)
        b, e0 = call(k_prev, [(2, 12), (2, 12)], zu, gain, b, e0, alias=[(2, 0), (3, 1)])
        e1, zpay = call(k_fine, [(2, 10), (8,)], w, wx, gain, b, e0)
        z1 = send(zpay, later)
        (e1,) = call(k_fine_prev, [(2, 10)], w, wx, gain, b, e0, z, e1, alias=[(6, 0)])
        part, pay = call(k_restrict, [(8,), (10,)], w, wx, diag, b, e1, cm)
        cm_twin = send(pay, twin)
        wm, wxm, diagm, gainm = call(k_mid_faces, [(4, 10), (11,), (10,), (10,)], cm)
        bm, m0, pay, ipay = call(
            k_restrict_prev, [(8,), (8,), (2,), (1,)], part, z1, gainm
        )
        z = send(m0, later)
        edge = send(pay, outer)
        near = gather(ipay, in_chip)
        (m1,) = call(k_mid, [(9,)], wm, wxm, gainm, bm, m0, near, cm_twin, far=(6,))
        m1, zpay, ipay = call(
            k_mid_prev, [(9,), (9,), (9,)], wm, wxm, gainm, bm, m0, edge, z, m1, b,
            alias=[(7, 0)],
        )
        z = send(zpay, later)
        near = gather(ipay, in_chip)
        residual, ct = call(k_residual_out, [(16,), (10,)], b, near, cm, cm_twin)
        wt, wxt, gaint = call(k_top_faces, [(4, 8), (9,), (8,)], ct)
        (rm,) = call(k_mid_left, [(8,)], wm, wxm, diagm, bm, m1, near)
        (rm,) = call(
            k_mid_left_prev, [(8,)], wm, wxm, diagm, gainm, bm, m1, z, rm, alias=[(7, 0)]
        )
        rms = gather(rm, twins)
        bt, t0, pay, ipay = call(k_top_start, [(8,), (8,), (1,), (1,)], gaint, rms)
        z = send(t0, later2)
        edge = send(pay, outer)
        near = gather(ipay, in_chip)
        mine, other = call(
            k_top, [(8,), (8,)], wt, wxt, gaint, bt, t0, near, m1, e1
        )
        mine, other = call(
            k_top_prev, [(8,), (8,)], wt, wxt, gaint, bt, t0, edge, z, m1, e1, mine, other,
            alias=[(9, 0), (10, 1)],
        )
        got = gather(other, in_chip)
        new = pl.pallas_call(
            k_state,
            out_shape=jax.ShapeDtypeStruct((16, 16, 512), jnp.float32),
            in_specs=[VMEM, VMEM, VMEM],
            out_specs=HBM,
            scratch_shapes=[
                pltpu.VMEM((16, 16, 512), jnp.float32),
                pltpu.SemaphoreType.DMA((4,)),
            ],
            compiler_params=pltpu.CompilerParams(vmem_limit_bytes=24 * 2**20),
            name="k_state",
        )(u_in, mine, got)
        return new[None, None], residual[None, None]

    spec = P("tm", "space", None, None, None)
    return jax.shard_map(
        shards,
        mesh=mesh,
        in_specs=(spec, spec, P("space", None, None, None)),
        out_specs=(spec, spec),
        check_vma=False,
    )
```
